32 devices in a mesh: dp: 8 (over z, y), tensor: 4 (over x, core).
Axes of the slice: x: 2, y: 2, z: 4, core: 2. Of those that a mesh axis runs over, the one named last changes fastest.
Arguments:
- tokens: bfloat16 [16384, 768], P(('dp', 'tensor')), may hold values from -6 to 6
- lengths: int32 [8, 8], P('dp'), may hold values from 0 to 1365, as said below
- cotangent: bfloat16 [16384, 768], P(('dp', 'tensor')), may hold values from -6 to 6
- ln1_gain: bfloat16 [768], P(('dp', 'tensor')), may hold values from 0.25 to 1.75
- ln1_bias: bfloat16 [768], P(('dp', 'tensor')), may hold values from -4 to 4
- w_qkv: bfloat16 [3, 768, 768], P(None, 'dp', 'tensor'), may hold values from -0.3125 to 0.3125
- b_qv: bfloat16 [2, 768], P(None, ('tensor', 'dp')), may hold values from -6 to 6
- w_out: bfloat16 [768, 768], P('tensor', 'dp'), may hold values from -0.875 to 0.875
- b_out: bfloat16 [768], P(('dp', 'tensor')), may hold values from -4 to 4
- ln2_gain: bfloat16 [768], P(('dp', 'tensor')), may hold values from 0.25 to 1.75
- ln2_bias: bfloat16 [768], P(('dp', 'tensor')), may hold values from -4 to 4
- w_fc1: bfloat16 [768, 3072], P('dp', 'tensor'), may hold values from -0.21875 to 0.21875
- b_fc1: bfloat16 [3072], P(('tensor', 'dp')), may hold values from -6 to 6
- w_fc2: bfloat16 [3072, 768], P('tensor', 'dp'), may hold values from -0.109375 to 0.109375
- b_fc2: bfloat16 [768], P(('dp', 'tensor')), may hold values from -4 to 4
Outputs:
- mixed: bfloat16 [16384, 768], P(('dp', 'tensor'))
- input_grad: bfloat16 [16384, 768], P(('dp', 'tensor'))
- grad_ln1_gain: float32 [768], P(('dp', 'tensor'))
- grad_ln1_bias: float32 [768], P(('dp', 'tensor'))
- grad_w_qkv: float32 [3, 768, 768], P(None, 'dp', 'tensor')
- grad_b_qv: float32 [2, 768], P(None, ('tensor', 'dp'))
- grad_w_out: float32 [768, 768], P('tensor', 'dp')
- grad_b_out: float32 [768], P(('dp', 'tensor'))
- grad_ln2_gain: float32 [768], P(('dp', 'tensor'))
- grad_ln2_bias: float32 [768], P(('dp', 'tensor'))
- grad_w_fc1: float32 [768, 3072], P('dp', 'tensor')
- grad_b_fc1: float32 [3072], P(('tensor', 'dp'))
- grad_w_fc2: float32 [3072, 768], P('tensor', 'dp')
- grad_b_fc2: float32 [768], P(('dp', 'tensor'))
The draws below stay inside these ranges and needn't reach their ends.
Inputs may be any that keep to these rules, and one draw needn't show every extreme that they name: Each row holds the lengths of the 8 documents of one group in order and sums to 2048. Entry 4 is the row's longest document: longer than 1024, starting before slot 512 and reaching slot 1536. Other entries may be 0.
All inputs are finite; a program needn't handle non-finite values.
Results may differ from the reference program's by a relative error of at most 0.02.
Values may be sent and summed in bfloat16 or wider, within the bound.
A program may use at most 128 MiB of HBM per device.

```python
import jax
import jax.numpy as jnp
from jax import lax

D = 768
HEADS = 12
HEAD_DIM = 64
FF = 3072
SLOTS = 2048
GROUPS = 1
QBLOCK = 512
DOCS = 8
MAXLEN = 1365
TOKENS = 16384
N_DP = 8
N_TENSOR = 4


def split_total(key, total, count):
    cuts = jax.random.randint(key, (total.shape[0], count - 1), 0, 1 << 20) % (total[:, None] + 1)
    cuts = jnp.sort(cuts, axis=1)
    zeros = jnp.zeros((total.shape[0], 1), jnp.int32)
    edges = jnp.concatenate([zeros, cuts.astype(jnp.int32), total[:, None].astype(jnp.int32)], axis=1)
    return edges[:, 1:] - edges[:, :-1]


def draw_lengths(key, part):
    key = jax.random.fold_in(key, 7)
    keys = jax.random.split(key, 5)
    rows_all = N_DP * GROUPS
    quarter = SLOTS // 4
    longest = jax.random.randint(keys[0], (rows_all,), SLOTS // 2 + 2, MAXLEN + 1)
    chosen = jax.random.randint(keys[1], (), 0, rows_all)
    longest = jnp.where(jnp.arange(rows_all) == chosen, MAXLEN, longest).astype(jnp.int32)
    low_start = jnp.maximum(0, 3 * quarter + 1 - longest)
    high_start = jnp.minimum(quarter - 1, SLOTS - longest)
    start = low_start + jax.random.randint(keys[2], (rows_all,), 0, 1 << 20) % (high_start - low_start + 1)
    tail = SLOTS - start - longest
    head_docs = split_total(keys[3], start.astype(jnp.int32), DOCS // 2)
    tail_docs = split_total(keys[4], tail.astype(jnp.int32), DOCS - 1 - DOCS // 2)
    return jnp.concatenate([head_docs, longest[:, None], tail_docs], axis=1).astype(jnp.int32)


def steps_of(key, shape, cuts, smallest, largest):
    def one(dim, blocks):
        steps = jax.random.uniform(jax.random.fold_in(jax.random.fold_in(key, 6), dim), (blocks,), jnp.float32, smallest / len(cuts), largest / len(cuts))
        return jnp.repeat(jnp.exp(steps), shape[dim] // blocks).reshape((-1,) + (1,) * (len(shape) - dim - 1))

    loudness = one(*cuts[0])
    for cut in cuts[1:]:
        loudness = loudness * one(*cut)
    return loudness


def normal_values(rng, extent, scale, reach, pieces=(), kind=jnp.bfloat16):
    drawn = scale * jax.random.normal(rng, extent, jnp.float32)
    if pieces:
        drawn = drawn * steps_of(rng, extent, pieces, -0.22, 0.18)
    return jnp.clip(drawn, -reach, reach).astype(kind)


def setup_inputs(seed: int = 0) -> dict:
    seeds = jax.random.split(jax.random.key(seed), 16)
    return {
        "tokens": normal_values(seeds[0], (TOKENS, D), 1.0, 6.0, ((0, 32),)),
        "lengths": draw_lengths(jax.random.fold_in(seeds[15], 71), 0),
        "cotangent": normal_values(seeds[2], (TOKENS, D), 1.0, 6.0, ((0, 32),)),
        "ln1_gain": jnp.clip(1.0 + 0.15 * jax.random.normal(seeds[3], (D,), jnp.float32), 0.25, 1.75).astype(jnp.bfloat16),
        "ln1_bias": normal_values(seeds[4], (D,), 0.3, 4.0, ((0, 32),)),
        "w_qkv": normal_values(seeds[5], (3, D, D), (D // 2) ** -0.5, 0.3125, ((1, 8), (2, 4))),
        "b_qv": normal_values(seeds[6], (2, D), 0.5, 6.0, ((1, 32),)),
        "w_out": normal_values(seeds[7], (D, D), (D // 16) ** -0.5, 0.875, ((0, 4), (1, 8))),
        "b_out": normal_values(seeds[8], (D,), 0.3, 4.0, ((0, 32),)),
        "ln2_gain": jnp.clip(1.0 + 0.15 * jax.random.normal(seeds[9], (D,), jnp.float32), 0.25, 1.75).astype(jnp.bfloat16),
        "ln2_bias": normal_values(seeds[10], (D,), 0.3, 4.0, ((0, 32),)),
        "w_fc1": normal_values(seeds[11], (D, FF), D ** -0.5, 0.21875, ((0, 8), (1, 4))),
        "b_fc1": normal_values(seeds[12], (FF,), 0.5, 6.0, ((0, 32),)),
        "w_fc2": normal_values(seeds[13], (FF, D), FF ** -0.5, 0.109375, ((0, 4), (1, 8))),
        "b_fc2": normal_values(seeds[14], (D,), 0.3, 4.0, ((0, 32),)),
    }


@jax.custom_vjp
def low(v):
    return lax.optimization_barrier(v.astype(jnp.bfloat16)).astype(jnp.float32)

@jax.custom_vjp
def low_back(v):
    return v

def low_keep(v):
    return (low(v), None)

def low_pass(kept, grad):
    return (grad,)

def back_keep(v):
    return (v, None)

def back_low(kept, grad):
    return (low(grad),)
low.defvjp(low_keep, low_pass)
low_back.defvjp(back_keep, back_low)
EPS = 1e-05
NEG = -1e+30

def both_ways(v):
    return low(low_back(v))

def mult(left, right):
    return jnp.dot(left, right, precision=lax.Precision.HIGHEST, preferred_element_type=jnp.float32)

def layer_norm(v, gain, shift):
    mean = lax.optimization_barrier(jnp.mean(v, axis=-1, keepdims=True))
    centered = v - mean
    spread = lax.optimization_barrier(jnp.mean(centered * centered, axis=-1, keepdims=True))
    return centered * lax.rsqrt(spread + EPS) * gain + shift

def doc_numbers(lengths):
    ends = jnp.cumsum(lengths, axis=-1).astype(jnp.int32)
    places = jnp.arange(SLOTS, dtype=jnp.int32)
    return lax.optimization_barrier(jnp.sum((ends[:, None, :] <= places[None, :, None]).astype(jnp.int32), axis=-1))

def head_attention(query, keys, values, segment):
    count = SLOTS // QBLOCK
    places = jnp.arange(SLOTS, dtype=jnp.int32)

    def block(index):
        start = index * QBLOCK
        qpart = lax.dynamic_slice_in_dim(query, start, QBLOCK, 0)
        rows = start + jnp.arange(QBLOCK, dtype=jnp.int32)
        qseg = lax.dynamic_slice_in_dim(segment, start, QBLOCK, 0)
        scores = jnp.einsum('qhd,khd->hqk', qpart, keys, precision=lax.Precision.HIGHEST)
        scores = low_back(scores) * 0.125
        allowed = (places[None, :] <= rows[:, None]) & (segment[None, :] == qseg[:, None])
        scores = jnp.where(allowed[None], scores, NEG)
        top = lax.optimization_barrier(jnp.max(scores, axis=-1, keepdims=True))
        weights = jnp.exp(scores - top)
        weights = weights / lax.optimization_barrier(jnp.sum(weights, axis=-1, keepdims=True))
        return jnp.einsum('hqk,khd->qhd', low(weights), values, precision=lax.Precision.HIGHEST)
    outs = lax.map(jax.checkpoint(block), jnp.arange(count, dtype=jnp.int32))
    return outs.reshape(SLOTS, query.shape[1], query.shape[2])

def group_forward(group_rows, segment, params):
    gain_one, bias_one, w_qkv, b_qv, w_out, b_out, gain_two, bias_two, w_fc1, b_fc1, w_fc2, b_fc2 = params
    width = D // N_TENSOR
    local_heads = HEADS // N_TENSOR
    normed_one = low(layer_norm(group_rows, gain_one, bias_one))
    attn_sum = jnp.zeros((SLOTS, D), jnp.float32)
    for group in range(N_TENSOR):
        first = group * width
        shared = low_back(normed_one)
        query = both_ways(mult(shared, w_qkv[0][:, first:first + width]) + b_qv[0][first:first + width])
        keys = both_ways(mult(shared, w_qkv[1][:, first:first + width]))
        values = both_ways(mult(shared, w_qkv[2][:, first:first + width]) + b_qv[1][first:first + width])
        shape = (SLOTS, local_heads, HEAD_DIM)
        attended = head_attention(query.reshape(shape), keys.reshape(shape), values.reshape(shape), segment)
        attended = both_ways(attended.reshape(SLOTS, width))
        attn_sum = attn_sum + low(mult(attended, w_out[first:first + width, :]))
    mid = group_rows + low_back(attn_sum) + b_out
    normed_two = low(layer_norm(mid, gain_two, bias_two))
    hidden_width = FF // N_TENSOR
    ff_sum = jnp.zeros((SLOTS, D), jnp.float32)
    for group in range(N_TENSOR):
        first = group * hidden_width
        shared = low_back(normed_two)
        pre = low_back(mult(shared, w_fc1[:, first:first + hidden_width]) + b_fc1[first:first + hidden_width])
        hid = low(jax.nn.gelu(pre, approximate=False))
        ff_sum = ff_sum + low(mult(hid, w_fc2[first:first + hidden_width, :]))
    return mid + low_back(ff_sum) + b_fc2

def reference(tokens, lengths, cotangent, ln1_gain, ln1_bias, w_qkv, b_qv, w_out, b_out, ln2_gain, ln2_bias, w_fc1, b_fc1, w_fc2, b_fc2):
    params = tuple((p.astype(jnp.float32) for p in (ln1_gain, ln1_bias, w_qkv, b_qv, w_out, b_out, ln2_gain, ln2_bias, w_fc1, b_fc1, w_fc2, b_fc2)))
    segments = doc_numbers(lengths)

    def forward(inputs, weights):
        grouped = inputs.reshape(N_DP * GROUPS, SLOTS, D)
        result = lax.map(lambda pair: group_forward(pair[0], pair[1], weights), (grouped, segments))
        return result.reshape(N_DP * GROUPS * SLOTS, D)
    result, pull = jax.vjp(forward, tokens.astype(jnp.float32), params)
    grad_tokens, grads = pull(cotangent.astype(jnp.float32))
    return (result.astype(jnp.bfloat16), grad_tokens.astype(jnp.bfloat16), grads[0], grads[1], grads[2], grads[3], grads[4], grads[5], grads[6], grads[7], grads[8], grads[9], grads[10], grads[11])
```

```python
import jax
import jax.numpy as jnp
from jax import lax
from jax.sharding import PartitionSpec as P

HEAD_DIM = 64
SLOTS = 2048
BLOCK = 512
EPS = 1e-05
NEG = -1e30


def matmul(left, right):
    return jnp.dot(left, right, preferred_element_type=jnp.float32)


def transpose_dot(left, right):
    return lax.dot_general(
        left, right, (((0,), (0,)), ((), ())), preferred_element_type=jnp.float32
    )


def dot_rows(left, right):
    return lax.dot_general(
        left, right, (((1,), (1,)), ((), ())), preferred_element_type=jnp.float32
    )


def split_heads(x):
    total, width = x.shape
    return x.reshape(total, width // HEAD_DIM, HEAD_DIM).transpose(1, 0, 2)


def join_heads(x):
    return x.transpose(1, 0, 2).reshape(x.shape[1], -1)


def head_dot(spec, left, right):
    return jnp.einsum(spec, left, right, preferred_element_type=jnp.float32)


def masked_scores(query, keys, starts, begin):
    scores = head_dot("hqd,hkd->hqk", query, keys)
    rows = begin + lax.broadcasted_iota(jnp.int32, scores.shape[1:], 0)
    cols = lax.broadcasted_iota(jnp.int32, scores.shape[1:], 1)
    low = starts[begin : begin + BLOCK, None]
    return jnp.where(((cols >= low) & (cols <= rows))[None], scores, NEG)


def attend(starts, query, keys, values):
    outs, logs = [], []
    for begin in range(0, SLOTS, BLOCK):
        end = begin + BLOCK
        scores = masked_scores(query[:, begin:end], keys[:, :end], starts, begin)
        top = jnp.max(scores, axis=2, keepdims=True)
        weights = jnp.exp(scores - top)
        summed = jnp.sum(weights, axis=2, keepdims=True)
        out = head_dot("hqk,hkd->hqd", weights.astype(jnp.bfloat16), values[:, :end])
        outs.append((out / summed).astype(jnp.bfloat16))
        logs.append(top + jnp.log(summed))
    return jnp.concatenate(outs, axis=1), logs


def attend_back(starts, query, keys, values, grad, out, logs):
    inner = jnp.sum(grad.astype(jnp.float32) * out.astype(jnp.float32), axis=2, keepdims=True)
    grad_query, grad_keys, grad_values = [], 0.0, 0.0
    for step in reversed(range(SLOTS // BLOCK)):
        begin, end = step * BLOCK, (step + 1) * BLOCK
        q, g = query[:, begin:end], grad[:, begin:end]
        scores = masked_scores(q, keys[:, :end], starts, begin)
        probs = jnp.exp(scores - logs[step])
        dprobs = head_dot("hqd,hkd->hqk", g, values[:, :end])
        dscores = (probs * (dprobs - inner[:, begin:end])).astype(jnp.bfloat16)
        probs = probs.astype(jnp.bfloat16)
        grad_query.append(head_dot("hqk,hkd->hqd", dscores, keys[:, :end]) * 0.125)
        pad = ((0, 0), (0, SLOTS - end), (0, 0))
        grad_keys += jnp.pad(head_dot("hqk,hqd->hkd", dscores, q), pad)
        grad_values += jnp.pad(head_dot("hqk,hqd->hkd", probs, g), pad)
    grad_query = jnp.concatenate(grad_query[::-1], axis=1)
    parts = [join_heads(x.astype(jnp.bfloat16)) for x in (grad_query, grad_keys, grad_values)]
    return jnp.concatenate(parts, axis=1)


def feed(x, g, w1, b1, w2t):
    pre = matmul(x, w1) + b1
    half = 0.5 * (1.0 + lax.erf(pre * 0.7071067811865476))
    slope = half + pre * jnp.exp(-0.5 * pre * pre) * 0.3989422804014327
    hid = (pre * half).astype(jnp.bfloat16)
    hid, slope = lax.optimization_barrier((hid, slope))
    gp = (matmul(g, w2t) * slope).astype(jnp.bfloat16)
    gp = lax.optimization_barrier(gp)
    pieces = dot_rows(hid, w2t).astype(jnp.bfloat16)
    grad_pieces = dot_rows(gp, w1).astype(jnp.bfloat16)
    dw = jnp.concatenate(
        [transpose_dot(x, gp).astype(jnp.bfloat16), transpose_dot(g, hid).astype(jnp.bfloat16)],
        axis=1,
    )
    return pieces, grad_pieces, dw, jnp.sum(gp.astype(jnp.float32), axis=0)


FAR = [(t, t ^ 2) for t in range(4)]
PEER = [(t, t ^ 1) for t in range(4)]


def far(x):
    return lax.ppermute(x, "tensor", FAR)


def peer(x):
    return lax.ppermute(x, "tensor", PEER)


def gathered_pair(x):
    mine = jnp.stack([x, far(x)])
    return mine, peer(mine)


def gathered_mine_first(x):
    mine, theirs = gathered_pair(x)
    return jnp.concatenate([mine, theirs]).reshape(-1, x.shape[-1])


def gathered_in_order(x):
    mine, theirs = gathered_pair(x)
    index = lax.axis_index("tensor")
    chip, core = index // 2, index % 2
    near = jnp.where(core == 0, jnp.stack([mine, theirs], 1), jnp.stack([theirs, mine], 1))
    return jnp.where(chip == 0, near, near[::-1]).reshape(-1, x.shape[-1])


def summed_pair(keep, away):
    got = peer(away)
    other = (keep[1].astype(jnp.float32) + got[1].astype(jnp.float32)).astype(jnp.bfloat16)
    back = far(other)
    return keep[0].astype(jnp.float32) + got[0].astype(jnp.float32) + back.astype(jnp.float32)


def summed_mine_first(x):
    x = x.reshape(2, 2, -1, x.shape[-1])
    return summed_pair(x[0], x[1])


def summed_in_order(x):
    index = lax.axis_index("tensor")
    chip, core = index // 2, index % 2
    x = x.reshape(2, 2, -1, x.shape[-1])
    keep = lax.dynamic_index_in_dim(x, core, 1, keepdims=False)
    away = lax.dynamic_index_in_dim(x, 1 - core, 1, keepdims=False)
    return summed_pair(
        jnp.where(chip == 0, keep, keep[::-1]), jnp.where(chip == 0, away, away[::-1])
    )


def exchanged(x, axis):
    return lax.all_to_all(x, axis, 0, 0, tiled=True)


def spread_to_all(x, axis, count):
    return exchanged(jnp.broadcast_to(x[None], (count,) + x.shape), axis)


def summed_blocks(x, axis, count):
    blocks = exchanged(x.reshape(count, -1, x.shape[-1]), axis)
    return jnp.sum(blocks.astype(jnp.float32), axis=0)


def norm_parts(v):
    mean = jnp.mean(v, axis=-1, keepdims=True)
    centered = v - mean
    r = lax.rsqrt(jnp.mean(centered * centered, axis=-1, keepdims=True) + EPS)
    return centered * r, r


def norm_back(e, gain, vhat, r):
    u = e * gain
    return r * (
        u
        - jnp.mean(u, axis=-1, keepdims=True)
        - vhat * jnp.mean(u * vhat, axis=-1, keepdims=True)
    )


def local(
    tokens,
    lengths,
    cotangent,
    ln1_gain,
    ln1_bias,
    w_qkv,
    b_qv,
    w_out,
    b_out,
    ln2_gain,
    ln2_bias,
    w_fc1,
    b_fc1,
    w_fc2,
    b_fc2,
):
    n_dp = lax.axis_size("dp")
    n_tp = lax.axis_size("tensor")
    index = lax.axis_index("tensor")
    both = ("dp", "tensor")
    model = tokens.shape[1]
    width = w_out.shape[0]
    shard = model // n_dp
    piece_v = ln1_gain.shape[0]
    piece_b = b_qv.shape[1]
    piece_f = b_fc1.shape[0]

    ends = jnp.cumsum(lengths[0])
    places = jnp.arange(SLOTS, dtype=jnp.int32)
    starts = jnp.max(jnp.where(ends[None, :] <= places[:, None], ends[None, :], 0), axis=1)

    small = jnp.concatenate(
        [ln1_gain, ln1_bias, b_out, ln2_gain, ln2_bias, b_fc2, b_qv.reshape(-1), b_fc1]
    )
    small = jnp.pad(small, (0, -small.shape[0] % 128)).reshape(1, -1).astype(jnp.float32)
    small = spread_to_all(small, both, n_dp * n_tp)[:, 0]
    gain_one, bias_one, out_bias, gain_two, bias_two, ff_bias = [
        small[:, k * piece_v : (k + 1) * piece_v].reshape(-1) for k in range(6)
    ]
    group = lax.dynamic_index_in_dim(small.reshape(n_dp, n_tp, -1), index, 1, keepdims=False)
    at = 6 * piece_v
    b_query = group[:, at : at + piece_b].reshape(-1)
    b_value = group[:, at + piece_b : at + 2 * piece_b].reshape(-1)
    ff_mid_bias = group[:, at + 2 * piece_b : at + 2 * piece_b + piece_f].reshape(1, -1)
    qkv_bias = jnp.concatenate([b_query, jnp.zeros_like(b_query), b_value])

    qkv_shard = w_qkv.transpose(1, 0, 2).reshape(shard, 3 * width)
    att_qkv = spread_to_all(qkv_shard, "dp", n_dp).reshape(model, 3 * width)

    whole_tokens = gathered_in_order(tokens)
    out_rows = spread_to_all(w_out, "tensor", n_tp).reshape(model, shard)
    rest, _ = lax.optimization_barrier(
        (jnp.concatenate([out_rows.T, w_fc1, w_fc2.T], axis=1), att_qkv)
    )
    rest = lax.all_gather(rest, "dp", axis=0, tiled=True)
    att_out_t = rest[:, :model]
    hidden = w_fc1.shape[1]
    ff_first = rest[:, model : model + hidden]
    ff_second_t = rest[:, model + hidden :]

    vhat_all, _ = norm_parts(whole_tokens.astype(jnp.float32))
    whole_one = (vhat_all * gain_one + bias_one).astype(jnp.bfloat16)
    qkv = (matmul(whole_one, att_qkv) + qkv_bias).astype(jnp.bfloat16)
    cot_low, _ = lax.optimization_barrier((cotangent, qkv))
    grad_whole = gathered_mine_first(cot_low)

    query = split_heads(qkv[:, :width] * jnp.bfloat16(0.125))
    keys = split_heads(qkv[:, width : 2 * width])
    values = split_heads(qkv[:, 2 * width :])
    attended, lse = attend(starts, query, keys, values)
    rows = tokens.shape[0]
    heads_rows = exchanged(join_heads(attended).reshape(n_tp, rows, width), "tensor")
    heads_rows = jnp.moveaxis(heads_rows, 0, 1).reshape(rows, model)
    inputs = tokens.astype(jnp.float32)
    mid = inputs + dot_rows(heads_rows, att_out_t) + out_bias
    vhat_two, r_two = norm_parts(mid)
    low_two = (vhat_two * gain_two + bias_two).astype(jnp.bfloat16)
    whole_two = gathered_mine_first(low_two)

    pieces, grad_pieces, grad_ff, grad_mid_bias = feed(
        whole_two, grad_whole, ff_first, ff_mid_bias, ff_second_t
    )
    grad_two = summed_mine_first(grad_pieces)
    pieces, grad_ff, grad_two = lax.optimization_barrier((pieces, grad_ff, grad_two))
    grad_out = cotangent.astype(jnp.float32)
    grad_mid = grad_out + norm_back(grad_two, gain_two, vhat_two, r_two)
    grad_low = grad_mid.astype(jnp.bfloat16)
    grad_heads = matmul(grad_low, att_out_t).astype(jnp.bfloat16)
    grad_heads = jnp.moveaxis(grad_heads.reshape(rows, n_tp, width), 1, 0)
    grad_attended = exchanged(grad_heads, "tensor").reshape(-1, width)
    pieces, grad_ff, grad_attended = lax.optimization_barrier((pieces, grad_ff, grad_attended))

    mixed = mid + summed_mine_first(pieces) + ff_bias
    ff_sums = summed_blocks(grad_ff, "dp", n_dp)
    grad_out_t = transpose_dot(grad_low, heads_rows).astype(jnp.bfloat16)
    grad_out_t = jnp.moveaxis(grad_out_t.reshape(model, n_tp, width), 1, 0)
    grad_out_t = jnp.sum(exchanged(grad_out_t, "tensor").astype(jnp.float32), axis=0)

    grad_qkv = attend_back(
        starts, query, keys, values, split_heads(grad_attended), attended, lse
    )
    partial_one = dot_rows(grad_qkv, att_qkv)
    grad_one = summed_in_order(partial_one.astype(jnp.bfloat16))
    att_grads = jnp.concatenate(
        [transpose_dot(whole_one, grad_qkv).astype(jnp.bfloat16), grad_out_t.astype(jnp.bfloat16)],
        axis=1,
    )
    att_sums = summed_blocks(att_grads, "dp", n_dp)
    grad_qkv_w = att_sums[:, : 3 * width].reshape(shard, 3, width).transpose(1, 0, 2)
    grad_w_out = att_sums[:, 3 * width :].T

    grad_bias = jnp.sum(grad_qkv.astype(jnp.float32), axis=0)
    vectors = [
        jnp.sum(partial_one * vhat_all, axis=0),
        jnp.sum(partial_one, axis=0),
        jnp.sum(grad_mid, axis=0),
        jnp.sum(grad_two * vhat_two, axis=0),
        jnp.sum(grad_two, axis=0),
        jnp.sum(grad_out, axis=0),
    ]
    wide = jnp.stack([v.reshape(n_dp * n_tp, piece_v) for v in vectors], axis=1)
    wide = wide.reshape(n_dp, n_tp, 6 * piece_v)
    own = jnp.concatenate(
        [
            grad_bias[:width].reshape(n_dp, piece_b),
            grad_bias[2 * width :].reshape(n_dp, piece_b),
            grad_mid_bias.reshape(n_dp, piece_f),
        ],
        axis=1,
    )
    here = (jnp.arange(n_tp) == index)[None, :, None]
    own = jnp.where(here, own[:, None, :], 0.0)
    packed = jnp.concatenate([wide, own], axis=2)
    packed = jnp.pad(packed, ((0, 0), (0, 0), (0, -packed.shape[2] % 128)))
    sums = summed_blocks(packed.reshape(n_dp * n_tp, 1, -1), both, n_dp * n_tp)[0]
    vec = [sums[k * piece_v : (k + 1) * piece_v] for k in range(6)]
    grad_b_qv = sums[at : at + 2 * piece_b].reshape(2, piece_b)
    grad_b_fc1 = sums[at + 2 * piece_b : at + 2 * piece_b + piece_f]

    vhat_one, r_one = norm_parts(inputs)
    grad_tokens = grad_mid + norm_back(grad_one, gain_one, vhat_one, r_one)
    return (
        mixed.astype(jnp.bfloat16),
        grad_tokens.astype(jnp.bfloat16),
        vec[0],
        vec[1],
        grad_qkv_w,
        grad_b_qv,
        grad_w_out,
        vec[2],
        vec[3],
        vec[4],
        ff_sums[:, :hidden],
        grad_b_fc1,
        ff_sums[:, hidden:].T,
        vec[5],
    )


def solution(mesh):
    in_specs = (
        P(("dp", "tensor"), None),
        P("dp", None),
        P(("dp", "tensor"), None),
        P(("dp", "tensor")),
        P(("dp", "tensor")),
        P(None, "dp", "tensor"),
        P(None, ("tensor", "dp")),
        P("tensor", "dp"),
        P(("dp", "tensor")),
        P(("dp", "tensor")),
        P(("dp", "tensor")),
        P("dp", "tensor"),
        P(("tensor", "dp")),
        P("tensor", "dp"),
        P(("dp", "tensor")),
    )
    out_specs = (
        P(("dp", "tensor"), None),
        P(("dp", "tensor"), None),
        P(("dp", "tensor")),
        P(("dp", "tensor")),
        P(None, "dp", "tensor"),
        P(None, ("tensor", "dp")),
        P("tensor", "dp"),
        P(("dp", "tensor")),
        P(("dp", "tensor")),
        P(("dp", "tensor")),
        P("dp", "tensor"),
        P(("tensor", "dp")),
        P("tensor", "dp"),
        P(("dp", "tensor")),
    )
    return jax.shard_map(local, mesh=mesh, in_specs=in_specs, out_specs=out_specs, check_vma=False)
```
